32 devices in a mesh: group: 2 (over x), tile: 8 (over z, y), draw: 2 (over core).
Axes of the slice: x: 2, y: 2, z: 4, core: 2. Of those that a mesh axis runs over, the one named last changes fastest.
Arguments:
- inputs: bfloat16 [4, 32, 270, 256], P(('group', 'draw'), 'tile'), parts along dimension 0, may hold values from -6 to 6
- land_mask: int32 [32, 270], P('tile'), may hold values 0 or 1
- kernel: float32 [7, 7, 256], replicated, may hold values from -0.875 to 0.875
- conv_bias: float32 [256], replicated, may hold values from -3 to 3
- norm_gain: float32 [256], replicated, may hold values from 0.1 to 1.9
- norm_bias: float32 [256], replicated, may hold values from -3 to 3
- w_in: bfloat16 [256, 1024], replicated, may hold values from -0.375 to 0.375
- b_in: float32 [1024], replicated, may hold values from -3 to 3
- w_out: bfloat16 [1024, 256], replicated, may hold values from -0.1875 to 0.1875
- b_out: float32 [256], replicated, may hold values from -3 to 3
- layer_scale: float32 [256], replicated, may hold values from 0.1 to 1.9
- cotangent: bfloat16 [4, 32, 270, 256], P(('group', 'draw'), 'tile'), parts along dimension 0, may hold values from -6 to 6
Outputs:
- output: bfloat16 [4, 32, 270, 256], P(('group', 'draw'), 'tile'), parts along dimension 0
- input_grad: bfloat16 [4, 32, 270, 256], P(('group', 'draw'), 'tile'), parts along dimension 0
- kernel_grad: float32 [14, 7, 256], P('group'), parts along dimension 0
- w_in_grad: float32 [512, 1024], P('group'), parts along dimension 0
- w_out_grad: float32 [2048, 256], P('group'), parts along dimension 0
- b_in_grad: float32 [2048], P('group'), parts along dimension 0
- channel_grads: float32 [10, 256], P('group'), parts along dimension 0
The draws below stay inside these ranges and needn't reach their ends.
There are 2 independent parts, one for each index of `group`. The reference program is written for one: setup_inputs(seed, part) draws one part's arguments, and reference() takes and returns one part's arrays. A program takes and returns all parts, laid end to end along the dimension named above; an argument that names none is the same for every part. Nothing has to cross between parts.
All inputs are finite; a program needn't handle non-finite values. No bound on the sum of `land_mask` on one device may be relied on, other than what follows from the above.
Results may differ from the reference program's by a relative error of at most 0.007.
Values may be sent and summed in bfloat16 or wider, within the bound.
A program may use at most 64 MiB of HBM per device.

```python
import jax
import jax.numpy as jnp
from jax import lax

C = 256
HID = 1024
NLON = 270
NLAT = 32
NDRAW = 2


def touch_ends(array, own_key, least, top_value):
    longest = array.shape.index(max(array.shape))
    spots = []
    for shift in (0, 1):
        where = [jax.random.randint(jax.random.fold_in(own_key, axis), (), 0, length) for axis, length in enumerate(array.shape)]
        where[longest] = (where[longest] + shift) % array.shape[longest]
        spots.append(tuple(where))
    return array.at[spots[0]].set(least).at[spots[1]].set(top_value)


def steps_of(key, dims, pieces, least, high):
    def one(axis_at, shards_of):
        heights = jax.random.uniform(jax.random.fold_in(jax.random.fold_in(key, 6), axis_at), (shards_of,), jnp.float32, least / len(pieces), high / len(pieces))
        return jnp.repeat(jnp.exp(heights), dims[axis_at] // shards_of).reshape((-1,) + (1,) * (len(dims) - axis_at - 1))

    gain = one(*pieces[0])
    for cut in pieces[1:]:
        gain = gain * one(*cut)
    return gain


def bell_draw(rng, extent, width, reach, shards=(), held_as=jnp.bfloat16):
    gain = steps_of(rng, extent, shards, -0.22, 0.18) if shards else 1.0
    values = jax.random.normal(rng, extent, jnp.float32) * width * gain
    return jnp.minimum(jnp.maximum(values, -reach), reach).astype(held_as)


def setup_inputs(seed: int = 0, part: int = 0) -> dict:
    splits = jax.random.split(jax.random.key(seed), 13)
    part_keys = jax.random.split(jax.random.fold_in(splits[12], part), 13)
    return {
        "inputs": bell_draw(part_keys[0], (NDRAW, NLAT, NLON, C), 1.0, 6.0, ((0, 2), (1, 8))),
        "land_mask": touch_ends((jax.random.randint(splits[1], (NLAT, NLON), 0, 4) < 3).astype(jnp.int32), jax.random.fold_in(splits[1], 1), 0, 1),
        "kernel": bell_draw(splits[2], (7, 7, C), 49 ** -0.5, 0.875, (), jnp.float32),
        "conv_bias": bell_draw(splits[3], (C,), 0.5, 3.0, (), jnp.float32),
        "norm_gain": jnp.clip(1.0 + 0.18 * jax.random.normal(splits[4], (C,), jnp.float32), 0.1, 1.9),
        "norm_bias": bell_draw(splits[5], (C,), 0.5, 3.0, (), jnp.float32),
        "w_in": bell_draw(splits[6], (C, HID), C ** -0.5, 0.375),
        "b_in": bell_draw(splits[7], (HID,), 0.5, 3.0, (), jnp.float32),
        "w_out": bell_draw(splits[8], (HID, C), HID ** -0.5, 0.1875),
        "b_out": bell_draw(splits[9], (C,), 0.5, 3.0, (), jnp.float32),
        "layer_scale": jnp.clip(1.0 + 0.18 * jax.random.normal(splits[10], (C,), jnp.float32), 0.1, 1.9),
        "cotangent": bell_draw(part_keys[11], (NDRAW, NLAT, NLON, C), 1.0, 6.0, ((0, 2), (1, 8))),
    }


ROOT_TERM = 0.7978845608028654
CUBIC = 0.044715
EPSILON = 1e-06

def lon_wrap(values):
    return jnp.concatenate([values[:, :, -3:], values, values[:, :, :3]], axis=2)

def apply_taps(padded, weights, height, breadth):
    total = jnp.zeros((padded.shape[0], height, breadth, padded.shape[3]), jnp.float32)
    for row_off in range(7):
        for col_off in range(7):
            total = total + padded[:, row_off:row_off + height, col_off:col_off + breadth, :] * weights[row_off, col_off]
    return total

def kernel_terms(padded, grad_map, height, breadth):
    rows_list = []
    for row_off in range(7):
        cells_list = []
        for col_off in range(7):
            window = padded[:, row_off:row_off + height, col_off:col_off + breadth, :]
            cells_list.append(lax.optimization_barrier(jnp.sum(window * grad_map, axis=(0, 1, 2))))
        rows_list.append(jnp.stack(cells_list))
    return jnp.stack(rows_list)

def gelu_slope(hidden):
    inner = ROOT_TERM * (hidden + CUBIC * hidden * hidden * hidden)
    tanh_value = jnp.tanh(inner)
    return 0.5 * (1.0 + tanh_value) + 0.5 * hidden * (1.0 - tanh_value * tanh_value) * ROOT_TERM * (1.0 + 3.0 * CUBIC * hidden * hidden)

def forward_backward(state, padded_state, land_mask, kernel, conv_bias, norm_gain, norm_bias, w_in, b_in, w_out, b_out, layer_scale, cotangent, extend):
    height = state.shape[1]
    breadth = state.shape[2]
    channels = state.shape[3]
    wrapped = lon_wrap(padded_state.astype(jnp.float32))
    conv_out = apply_taps(wrapped, kernel, height, breadth) + conv_bias
    center = lax.optimization_barrier(jnp.mean(conv_out, axis=-1, keepdims=True))
    deviation = conv_out - center
    inv_std = lax.rsqrt(lax.optimization_barrier(jnp.mean(deviation * deviation, axis=-1, keepdims=True)) + EPSILON)
    unit = deviation * inv_std
    normed = (unit * norm_gain + norm_bias).astype(jnp.bfloat16).reshape(-1, channels)
    hidden = jnp.dot(normed, w_in, preferred_element_type=jnp.float32) + b_in
    inner = ROOT_TERM * (hidden + CUBIC * hidden * hidden * hidden)
    activated = (0.5 * hidden * (1.0 + jnp.tanh(inner))).astype(jnp.bfloat16)
    mixed = (jnp.dot(activated, w_out, preferred_element_type=jnp.float32) + b_out).reshape(state.shape)
    ocean = land_mask.astype(jnp.float32)[None, :, :, None]
    output = (state.astype(jnp.float32) + ocean * layer_scale * mixed).astype(jnp.bfloat16)
    upstream = cotangent.astype(jnp.float32)
    scale_part = lax.optimization_barrier(jnp.sum(ocean * upstream * mixed, axis=(0, 1, 2)))
    grad_mixed = (ocean * layer_scale * upstream).astype(jnp.bfloat16).reshape(-1, channels)
    out_bias_part = lax.optimization_barrier(jnp.sum(grad_mixed.astype(jnp.float32), axis=0))
    w_out_part = lax.dot_general(activated, grad_mixed, (((0,), (0,)), ((), ())), preferred_element_type=jnp.float32)
    grad_act = lax.dot_general(grad_mixed, w_out, (((1,), (1,)), ((), ())), preferred_element_type=jnp.float32)
    grad_hidden = (grad_act * gelu_slope(hidden)).astype(jnp.bfloat16)
    w_in_part = lax.dot_general(normed, grad_hidden, (((0,), (0,)), ((), ())), preferred_element_type=jnp.float32)
    hidden_bias_part = lax.optimization_barrier(jnp.sum(grad_hidden.astype(jnp.float32), axis=0))
    grad_normed = lax.dot_general(grad_hidden, w_in, (((1,), (1,)), ((), ())), preferred_element_type=jnp.float32).reshape(state.shape)
    gain_part = lax.optimization_barrier(jnp.sum(grad_normed * unit, axis=(0, 1, 2)))
    nbias_part = lax.optimization_barrier(jnp.sum(grad_normed, axis=(0, 1, 2)))
    scaled = grad_normed * norm_gain
    grad_conv = (inv_std * (scaled - lax.optimization_barrier(jnp.mean(scaled, axis=-1, keepdims=True)) - unit * lax.optimization_barrier(jnp.mean(scaled * unit, axis=-1, keepdims=True)))).astype(jnp.bfloat16)
    grad_float = grad_conv.astype(jnp.float32)
    conv_bias_part = lax.optimization_barrier(jnp.sum(grad_float, axis=(0, 1, 2)))
    kernel_part = kernel_terms(wrapped, grad_float, height, breadth)
    grad_padded = lon_wrap(extend(grad_conv).astype(jnp.float32))
    input_grad = (upstream + apply_taps(grad_padded, kernel[::-1, ::-1], height, breadth)).astype(jnp.bfloat16)
    channel_part = jnp.stack([conv_bias_part, gain_part, nbias_part, out_bias_part, scale_part])
    return (output, input_grad, kernel_part, w_in_part, w_out_part, hidden_bias_part, channel_part)

def lat_zeros(values):
    return jnp.pad(values, ((0, 0), (3, 3), (0, 0), (0, 0)))

def reference(inputs, land_mask, kernel, conv_bias, norm_gain, norm_bias, w_in, b_in, w_out, b_out, layer_scale, cotangent):
    results = forward_backward(inputs, lat_zeros(inputs), land_mask, kernel, conv_bias, norm_gain, norm_bias, w_in, b_in, w_out, b_out, layer_scale, cotangent, lat_zeros)
    output, input_grad, kernel_part, w_in_part, w_out_part, hidden_bias_part, channel_part = results
    factor = 1.0 / jnp.sqrt(jnp.float32(NDRAW * NLAT * NLON))
    return (output, input_grad, kernel_part * factor, w_in_part * factor, w_out_part * factor, hidden_bias_part * factor, channel_part * factor)
```

```python
import functools

import jax
import jax.numpy as jnp
from jax import lax
from jax.experimental import pallas as pl
from jax.experimental.pallas import tpu as pltpu
from jax.sharding import PartitionSpec as P

ROOT_TERM = 0.7978845608028654
CUBIC = 0.044715
EPSILON = 1e-06
F32 = jnp.float32
BF16 = jnp.bfloat16


def block_kernel(
    n,
    scale,
    x_ref,
    cot_ref,
    mask_ref,
    taps_ref,
    conv_bias_ref,
    gain_ref,
    nbias_ref,
    w_in_ref,
    b_in_ref,
    w_out_ref,
    b_out_ref,
    ls_ref,
    out_ref,
    igrad_ref,
    wi_ref,
    wo_ref,
    small_ref,
    xo,
    x_top,
    x_bot,
    cot,
    wrap,
    xs,
    gs,
    acc,
    hid,
    gact,
    act,
    gh,
    normed,
    gmix,
    gb,
    g_top,
    g_bot,
    gf,
    bsum,
    chan,
    part,
    r1,
    r2,
    r3,
    whole,
    sm,
    s1,
    s2,
    s3,
    s5,
    s6,
    halo_send,
    halo_recv,
    send_sem,
    recv_sem,
    z_send,
    z_recv,
):
    H, W, C = x_ref.shape
    Wp = xo.shape[1]
    B = Wp // 8
    HID = w_in_ref.shape[1]
    m = n // 2
    g = lax.axis_index("group")
    t = lax.axis_index("tile")
    d = lax.axis_index("draw")
    zz = t // 2
    yy = lax.rem(t, 2)
    ty = t + 1 - 2 * yy
    core = (g, t, 1 - d)
    beside = (g, ty, d)
    up = (g, lax.rem(t + n - 1, n), d)
    down = (g, lax.rem(t + 1, n), d)
    zpeer = [(g, 2 * lax.rem(zz + k, m) + yy, d) for k in range(m)]

    def remote(src, dst, ss, rs, dev):
        return pltpu.make_async_remote_copy(
            src_ref=src,
            dst_ref=dst,
            send_sem=ss,
            recv_sem=rs,
            device_id=dev,
            device_id_type=pl.DeviceIdType.MESH,
        )

    barrier = pltpu.get_barrier_semaphore()
    for dev in [core, up, down] + zpeer[1:]:
        pl.semaphore_signal(barrier, inc=1, device_id=dev, device_id_type=pl.DeviceIdType.MESH)
    for p in range(H):
        xo[p, 0:W] = x_ref[p]
        xo[p, W:Wp] = jnp.zeros((Wp - W, C), BF16)
    pl.semaphore_wait(barrier, m + 2)

    def halo(own, top, bot, at):
        to_up = remote(own.at[0:3], bot, halo_send.at[at], halo_recv.at[at], up)
        to_down = remote(own.at[H - 3 : H], top, halo_send.at[at + 1], halo_recv.at[at + 1], down)
        return to_up, to_down

    def halo_wait(pair, top, bot):
        to_up, to_down = pair

        @pl.when(t > 0)
        def _():
            to_up.wait_send()
            to_down.wait_recv()

        @pl.when(t < n - 1)
        def _():
            to_down.wait_send()
            to_up.wait_recv()

        @pl.when(t == 0)
        def _():
            top[...] = jnp.zeros_like(top)

        @pl.when(t == n - 1)
        def _():
            bot[...] = jnp.zeros_like(bot)

    x_halo = halo(xo, x_top, x_bot, 0)

    @pl.when(t > 0)
    def _():
        x_halo[0].start()

    @pl.when(t < n - 1)
    def _():
        x_halo[1].start()

    def spread(value, dst, row):
        v = value.astype(F32)
        wrap[8 : 8 + Wp] = v
        wrap[5:8] = v[W - 3 : W]
        wrap[8 + W : 16 + W] = v[0:8]
        for j in range(7):
            dst[j, row] = wrap[5 + j : 5 + j + Wp].reshape(B, 8, C)

    def own_spread(own, dst):
        @pl.loop(0, H)
        def _(r):
            spread(own[r], dst, r + 3)

    def halo_spread(top, bot, dst):
        @pl.loop(0, 3)
        def _(r):
            spread(top[r], dst, r)
            spread(bot[r], dst, r + H + 3)

    def conv(src, rows, flip, first):
        @pl.loop(0, B // 2)
        def _(c):
            q = pl.ds(c * 2, 2)
            sums = [None if first else acc[p, q] for p in range(H)]
            for j in range(7):
                for r in rows:
                    cells = src[j, r, q]
                    for p in range(H):
                        i = r - p
                        if 0 <= i < 7:
                            tap = (6 - i) * 7 + 6 - j if flip else i * 7 + j
                            term = cells * taps_ref[tap][None]
                            sums[p] = term if sums[p] is None else sums[p] + term
            for p in range(H):
                acc[p, q] = sums[p]

    own_rows = list(range(3, H + 3))
    halo_rows = [0, 1, 2] + list(range(H + 3, H + 6))
    own_spread(xo, xs)
    conv(xs, own_rows, False, True)
    for p in range(H):
        cot[p, 0:W] = cot_ref[p].astype(F32)
        cot[p, W:Wp] = jnp.zeros((Wp - W, C), F32)
    bsum[...] = jnp.zeros_like(bsum)
    chan[...] = jnp.zeros_like(chan)
    halo_wait(x_halo, x_top, x_bot)
    halo_spread(x_top, x_bot, xs)
    conv(xs, halo_rows, False, False)

    def rowsum(v):
        return jnp.sum(v, axis=0, keepdims=True)

    @pl.loop(0, H)
    def _(p):
        conv_out = acc[p].reshape(Wp, C) + conv_bias_ref[...]
        dev = conv_out - jnp.mean(conv_out, axis=-1, keepdims=True)
        rstd = lax.rsqrt(jnp.mean(dev * dev, axis=-1, keepdims=True) + EPSILON)
        unit = dev * rstd
        gf[p] = unit
        normed[p] = (unit * gain_ref[...] + nbias_ref[...]).astype(BF16)
        hid[...] = jnp.dot(normed[p], w_in_ref[...], preferred_element_type=F32)
        ocean = mask_ref[p].astype(F32)
        grad_mixed = (ocean * ls_ref[...] * cot[p]).astype(BF16)
        gmix[p] = grad_mixed
        gact[...] = lax.dot_general(
            grad_mixed, w_out_ref[...], (((1,), (1,)), ((), ())), preferred_element_type=F32
        )

        @pl.loop(0, Wp // 16)
        def _(c):
            q = pl.ds(pl.multiple_of(c * 16, 16), 16)
            h = hid[q] + b_in_ref[...]
            h2 = h * h
            th = jnp.tanh(ROOT_TERM * (h + CUBIC * h2 * h))
            half = 0.5 * (1.0 + th)
            act[p, q] = (h * half).astype(BF16)
            slope = half + 0.5 * h * (1.0 - th * th) * ROOT_TERM * (1.0 + 3.0 * CUBIC * h2)
            grad_hidden = (gact[q] * slope).astype(BF16)
            gh[p, q] = grad_hidden
            wide = grad_hidden.astype(F32)
            bsum[...] += wide[0:8] + wide[8:16]

        mixed = jnp.dot(act[p], w_out_ref[...], preferred_element_type=F32) + b_out_ref[...]
        out_ref[p] = (xo[p].astype(F32) + ocean * ls_ref[...] * mixed).astype(BF16)[0:W]
        grad_normed = lax.dot_general(
            gh[p], w_in_ref[...], (((1,), (1,)), ((), ())), preferred_element_type=F32
        )
        unit = gf[p]
        scaled = grad_normed * gain_ref[...]
        grad_conv = rstd * (
            scaled
            - jnp.mean(scaled, axis=-1, keepdims=True)
            - unit * jnp.mean(scaled * unit, axis=-1, keepdims=True)
        )
        rounded = grad_conv.astype(BF16)
        gb[p] = rounded
        chan[0:1] += rowsum(rounded.astype(F32))
        chan[1:2] += rowsum(grad_normed * unit)
        chan[2:3] += rowsum(grad_normed)
        chan[3:4] += rowsum(gmix[p].astype(F32))
        chan[4:5] += rowsum(ocean * cot[p] * mixed)

    g_halo = halo(gb, g_top, g_bot, 2)

    @pl.when(t > 0)
    def _():
        g_halo[0].start()

    @pl.when(t < n - 1)
    def _():
        g_halo[1].start()

    flat = H * Wp
    tiles = part.shape[0] * part.shape[1] * part.shape[2] * part.shape[3]
    T = part.shape[3]
    d_in = lax.dot_general(
        normed[...].reshape(flat, C),
        gh[...].reshape(flat, HID),
        (((0,), (0,)), ((), ())),
        preferred_element_type=F32,
    )
    per = C // 16
    for cb in range(HID // C):
        for rb in range(per):
            k = cb * per + rb
            part[k // (tiles // 2), k // (tiles // 4) % 2, k // T % m, k % T, 0:16] = d_in[
                rb * 16 : rb * 16 + 16, cb * C : cb * C + C
            ].astype(BF16)
    d_out = lax.dot_general(
        gmix[...].reshape(flat, C),
        act[...].reshape(flat, HID),
        (((0,), (0,)), ((), ())),
        preferred_element_type=F32,
    ).T
    for k in range(tiles):
        part[k // (tiles // 2), k // (tiles // 4) % 2, k // T % m, k % T, 16:32] = d_out[
            k * 16 : k * 16 + 16
        ].astype(BF16)

    step1 = remote(part.at[1 - d], r1, send_sem.at[0], recv_sem.at[0], core)
    step1.start()

    own_spread(gb, gs)
    conv(gs, own_rows, True, True)

    step1.wait()
    r1[...] = (part[d].astype(F32) + r1[...].astype(F32)).astype(BF16)
    step2 = remote(r1.at[1 - yy], r2, send_sem.at[1], recv_sem.at[1], beside)
    step2.start()

    for j in range(7):

        def tap_terms(c, sums):
            q = pl.ds(c * 2, 2)
            cells16 = pl.ds(pl.multiple_of(c * 16, 16), 16)
            grads = [gb[p, cells16].astype(F32).reshape(2, 8, C) for p in range(H)]
            sums = list(sums)
            for r in range(H + 6):
                cells = xs[j, r, q]
                for p in range(H):
                    i = r - p
                    if 0 <= i < 7:
                        term = cells * grads[p]
                        sums[i] = sums[i] + (term[0] + term[1])
            return tuple(sums)

        sums = lax.fori_loop(0, B // 2, tap_terms, tuple(jnp.zeros((8, C), F32) for _ in range(7)))
        for i in range(7):
            k = i * 7 + j
            sm[k // 32, k % 32 : k % 32 + 1] = rowsum(sums[i])
    hidden_sum = rowsum(bsum[...])
    for k in range(HID // C):
        sm[1, 17 + k : 18 + k] = hidden_sum[:, k * C : k * C + C]
    sm[1, 21:26] = chan[0:5]
    sm[1, 26:32] = jnp.zeros((6, C), F32)

    small1 = remote(sm.at[1 - d], s1, send_sem.at[4], recv_sem.at[4], core)
    small1.start()
    step2.wait()
    r2[...] = (r1[yy].astype(F32) + r2[...].astype(F32)).astype(BF16)
    step3 = [
        remote(r2.at[lax.rem(zz + k, m)], r3.at[k - 1], z_send.at[k - 1], z_recv.at[k - 1], zpeer[k])
        for k in range(1, m)
    ]
    for copy in step3:
        copy.start()
    small1.wait()
    s2[...] = sm[d] + s1[...]
    small2 = remote(s2, s3, send_sem.at[5], recv_sem.at[5], beside)
    small2.start()

    halo_wait(g_halo, g_top, g_bot)
    halo_spread(g_top, g_bot, gs)

    for copy in step3:
        copy.wait()
    total = r2[zz].astype(F32)
    for k in range(m - 1):
        total = total + r3[k].astype(F32)
    whole[d, yy, zz] = (total * scale).astype(BF16)
    mine = whole.at[d, yy, zz]
    step4 = [
        remote(mine, mine, z_send.at[m - 2 + k], z_recv.at[m - 2 + k], zpeer[k])
        for k in range(1, m)
    ]
    for copy in step4:
        copy.start()
    small2.wait()
    s5[zz] = s2[...] + s3[...]
    small3 = [
        remote(s5.at[zz], s5.at[zz], z_send.at[2 * m - 3 + k], z_recv.at[2 * m - 3 + k], zpeer[k])
        for k in range(1, m)
    ]
    for copy in small3:
        copy.start()

    conv(gs, halo_rows, True, False)

    for copy in step4:
        copy.wait()
    step5 = remote(
        whole.at[d, yy], whole.at[d, yy], send_sem.at[2], recv_sem.at[2], beside
    )
    step5.start()
    for copy in small3:
        copy.wait()
    small_total = s5[0]
    for k in range(1, m):
        small_total = small_total + s5[k]
    s6[d] = small_total * scale
    small4 = remote(s6.at[d], s6.at[d], send_sem.at[6], recv_sem.at[6], core)
    small4.start()
    for p in range(H):
        igrad_ref[p] = (cot[p] + acc[p].reshape(Wp, C)).astype(BF16)[0:W]
    step5.wait()
    step6 = remote(whole.at[d], whole.at[d], send_sem.at[3], recv_sem.at[3], core)
    step6.start()
    small4.wait()
    small_ref[...] = s6[...]
    step6.wait()
    for cb in range(HID // C):
        for rb in range(per):
            k = cb * per + rb
            wi_ref[rb * 16 : rb * 16 + 16, cb * C : cb * C + C] = whole[
                k // (tiles // 2), k // (tiles // 4) % 2, k // T % m, k % T, 0:16
            ].astype(F32)
    for k in range(tiles):
        wo_ref[k * 16 : k * 16 + 16] = whole[
            k // (tiles // 2), k // (tiles // 4) % 2, k // T % m, k % T, 16:32
        ].astype(F32)


def per_device(
    n,
    draws,
    inputs,
    land_mask,
    kernel,
    conv_bias,
    norm_gain,
    norm_bias,
    w_in,
    b_in,
    w_out,
    b_out,
    layer_scale,
    cotangent,
):
    _, H, W, C = inputs.shape
    HID = w_in.shape[1]
    Wp = (W + 15) // 16 * 16
    B = Wp // 8
    m = n // 2
    T = HID // 16 // (2 * n)
    scale = float(1.0 / (draws * H * n * W) ** 0.5)
    ocean = jnp.broadcast_to(
        jnp.pad(land_mask, ((0, 0), (0, Wp - W))).astype(BF16)[:, :, None], (H, Wp, C)
    )
    taps = jnp.broadcast_to(kernel.reshape(49, 1, C), (49, 8, C))
    vm = pl.BlockSpec(memory_space=pltpu.VMEM)
    scratch = [
        ((H, Wp, C), BF16),
        ((3, Wp, C), BF16),
        ((3, Wp, C), BF16),
        ((H, Wp, C), F32),
        ((Wp + 16, C), F32),
        ((7, H + 6, B, 8, C), F32),
        ((7, H + 6, B, 8, C), F32),
        ((H, B, 8, C), F32),
        ((Wp, HID), F32),
        ((Wp, HID), F32),
        ((H, Wp, HID), BF16),
        ((H, Wp, HID), BF16),
        ((H, Wp, C), BF16),
        ((H, Wp, C), BF16),
        ((H, Wp, C), BF16),
        ((3, Wp, C), BF16),
        ((3, Wp, C), BF16),
        ((H, Wp, C), F32),
        ((8, HID), F32),
        ((8, C), F32),
        ((2, 2, m, T, 32, C), BF16),
        ((2, m, T, 32, C), BF16),
        ((m, T, 32, C), BF16),
        ((m - 1, T, 32, C), BF16),
        ((2, 2, m, T, 32, C), BF16),
        ((2, 32, C), F32),
        ((32, C), F32),
        ((32, C), F32),
        ((32, C), F32),
        ((m, 32, C), F32),
        ((2, 32, C), F32),
    ]
    output, input_grad, w_in_grad, w_out_grad, small = pl.pallas_call(
        functools.partial(block_kernel, n, scale),
        out_shape=(
            jax.ShapeDtypeStruct((H, W, C), BF16),
            jax.ShapeDtypeStruct((H, W, C), BF16),
            jax.ShapeDtypeStruct((C, HID), F32),
            jax.ShapeDtypeStruct((HID, C), F32),
            jax.ShapeDtypeStruct((2, 32, C), F32),
        ),
        in_specs=[vm] * 12,
        out_specs=[vm] * 5,
        scratch_shapes=[pltpu.VMEM(shape, dtype) for shape, dtype in scratch]
        + [
            pltpu.SemaphoreType.DMA((4,)),
            pltpu.SemaphoreType.DMA((4,)),
            pltpu.SemaphoreType.DMA((7,)),
            pltpu.SemaphoreType.DMA((7,)),
            pltpu.SemaphoreType.DMA((3 * (m - 1),)),
            pltpu.SemaphoreType.DMA((3 * (m - 1),)),
        ],
        compiler_params=pltpu.CompilerParams(
            collective_id=0, has_side_effects=True, vmem_limit_bytes=62 * 1024 * 1024
        ),
    )(
        inputs[0],
        cotangent[0],
        ocean,
        taps,
        conv_bias[None],
        norm_gain[None],
        norm_bias[None],
        w_in,
        b_in[None],
        w_out,
        b_out[None],
        layer_scale[None],
    )
    rows = small.reshape(64, C)
    return (
        output[None],
        input_grad[None],
        rows[0:49].reshape(7, 7, C),
        w_in_grad,
        w_out_grad,
        rows[49 : 49 + HID // C].reshape(HID),
        rows[49 + HID // C : 54 + HID // C],
    )


def solution(mesh):
    field = P(("group", "draw"), "tile", None, None)
    placed = (field, P("tile", None)) + (P(),) * 9 + (field,)
    return jax.shard_map(
        functools.partial(per_device, mesh.shape["tile"], mesh.shape["draw"]),
        mesh=mesh,
        in_specs=placed,
        out_specs=(
            field,
            field,
            P("group", None, None),
            P("group", None),
            P("group", None),
            P("group"),
            P("group", None),
        ),
        check_vma=False,
    )
```

```python
import functools

import jax
import jax.numpy as jnp
from jax import lax
from jax.experimental import pallas as pl
from jax.experimental.pallas import tpu as pltpu
from jax.sharding import PartitionSpec as P

ROOT_TERM = 0.7978845608028654
CUBIC = 0.044715
EPSILON = 1e-06
F32 = jnp.float32
BF16 = jnp.bfloat16


def block_kernel(
    n,
    scale,
    x_ref,
    cot_ref,
    mask_ref,
    taps_ref,
    conv_bias_ref,
    gain_ref,
    nbias_ref,
    w_in_ref,
    b_in_ref,
    w_out_ref,
    b_out_ref,
    ls_ref,
    out_ref,
    igrad_ref,
    wi_ref,
    wo_ref,
    kgrad_ref,
    bgrad_ref,
    chan_ref,
    xo,
    x_top,
    x_bot,
    cot,
    wrap,
    xs,
    acc,
    hid,
    gact,
    act,
    gh,
    normed,
    gmix,
    gb,
    g_top,
    g_bot,
    gf,
    bsum,
    chan,
    part,
    r1,
    r2,
    r3,
    whole,
    sm,
    s1,
    s2,
    s3,
    s5,
    s6,
    halo_send,
    halo_recv,
    send_sem,
    recv_sem,
    z_send,
    z_recv,
):
    H, W, C = x_ref.shape
    Wp = xo.shape[1]
    B = Wp // 8
    HID = w_in_ref.shape[1]
    m = n // 2
    g = lax.axis_index("group")
    t = lax.axis_index("tile")
    d = lax.axis_index("draw")
    zz = t // 2
    yy = lax.rem(t, 2)
    ty = t + 1 - 2 * yy
    core = (g, t, 1 - d)
    beside = (g, ty, d)
    up = (g, lax.rem(t + n - 1, n), d)
    down = (g, lax.rem(t + 1, n), d)
    zpeer = [(g, 2 * lax.rem(zz + k, m) + yy, d) for k in range(m)]

    def remote(src, dst, ss, rs, dev):
        return pltpu.make_async_remote_copy(
            src_ref=src,
            dst_ref=dst,
            send_sem=ss,
            recv_sem=rs,
            device_id=dev,
            device_id_type=pl.DeviceIdType.MESH,
        )

    barrier = pltpu.get_barrier_semaphore()
    for dev in [core, up, down] + zpeer[1:]:
        pl.semaphore_signal(barrier, inc=1, device_id=dev, device_id_type=pl.DeviceIdType.MESH)
    for p in range(H):
        xo[p, 0:W] = x_ref[p]
        xo[p, W:Wp] = jnp.zeros((Wp - W, C), BF16)
    pl.semaphore_wait(barrier, m + 2)

    @pl.when(t == 0)
    def _():
        x_top[...] = jnp.zeros_like(x_top)
        g_top[...] = jnp.zeros_like(g_top)

    @pl.when(t == n - 1)
    def _():
        x_bot[...] = jnp.zeros_like(x_bot)
        g_bot[...] = jnp.zeros_like(g_bot)

    def to_up(own, bot, a, at):
        k = at + a
        return remote(own.at[a], bot.at[a], halo_send.at[k], halo_recv.at[k], up)

    def to_down(own, top, a, at):
        k = at + 3 + a
        return remote(own.at[H - 3 + a], top.at[a], halo_send.at[k], halo_recv.at[k], down)

    def halo_start(own, top, bot, at, ups, downs):
        @pl.when(t > 0)
        def _():
            for a in ups:
                to_up(own, bot, a, at).start()

        @pl.when(t < n - 1)
        def _():
            for a in downs:
                to_down(own, top, a, at).start()

    def halo_arrive(own, top, bot, at, ups, downs):
        @pl.when(t > 0)
        def _():
            for a in downs:
                to_down(own, top, a, at).wait_recv()

        @pl.when(t < n - 1)
        def _():
            for a in ups:
                to_up(own, bot, a, at).wait_recv()

    def halo_sent(own, top, bot, at):
        @pl.when(t > 0)
        def _():
            for a in range(3):
                to_up(own, bot, a, at).wait_send()

        @pl.when(t < n - 1)
        def _():
            for a in range(3):
                to_down(own, top, a, at).wait_send()

    x_side = (xo, x_top, x_bot, 0)
    g_side = (gb, g_top, g_bot, 6)
    for a in range(3):
        halo_start(*x_side, [a], [2 - a])

    def spread(value, dst, row):
        v = value.astype(F32)
        wrap[8 : 8 + Wp] = v
        wrap[5:8] = v[W - 3 : W]
        wrap[8 + W : 16 + W] = v[0:8]
        for j in range(7):
            dst[j, row] = wrap[5 + j : 5 + j + Wp].reshape(B, 8, C)

    def own_spread(own, dst):
        @pl.loop(0, H)
        def _(r):
            spread(own[r], dst, r + 3)

    def halo_spread(top, bot, dst, ups, downs):
        for a in downs:
            spread(top[a], dst, a)
        for a in ups:
            spread(bot[a], dst, a + H + 3)

    def conv(src, rows, flip, first):
        @pl.loop(0, B // 2)
        def _(c):
            q = pl.ds(c * 2, 2)
            live = [p for p in range(H) if any(0 <= r - p < 7 for r in rows)]
            sums = [acc[p, q] if p in live and not first else None for p in range(H)]
            for j in range(7):
                for r in rows:
                    cells = src[j, r, q]
                    for p in range(H):
                        i = r - p
                        if 0 <= i < 7:
                            tap = (6 - i) * 7 + 6 - j if flip else i * 7 + j
                            term = cells * taps_ref[tap][None]
                            sums[p] = term if sums[p] is None else sums[p] + term
            for p in live:
                acc[p, q] = sums[p]

    own_rows = list(range(3, H + 3))
    own_spread(xo, xs)
    conv(xs, own_rows, False, True)
    for p in range(H):
        cot[p, 0:W] = cot_ref[p].astype(F32)
        cot[p, W:Wp] = jnp.zeros((Wp - W, C), F32)
    bsum[...] = jnp.zeros_like(bsum)
    chan[...] = jnp.zeros_like(chan)
    for a in range(2):
        halo_arrive(*x_side, [a], [2 - a])
        halo_spread(x_top, x_bot, xs, [a], [2 - a])
    conv(xs, [1, 2, H + 3, H + 4], False, False)

    def rowsum(v):
        return jnp.sum(v, axis=0, keepdims=True)

    def pointwise(p):
        conv_out = acc[p].reshape(Wp, C) + conv_bias_ref[...]
        dev = conv_out - jnp.mean(conv_out, axis=-1, keepdims=True)
        rstd = lax.rsqrt(jnp.mean(dev * dev, axis=-1, keepdims=True) + EPSILON)
        unit = dev * rstd
        gf[p] = unit
        normed[p] = (unit * gain_ref[...] + nbias_ref[...]).astype(BF16)
        hid[...] = jnp.dot(normed[p], w_in_ref[...], preferred_element_type=F32)
        ocean = mask_ref[p].astype(F32)
        grad_mixed = (ocean * ls_ref[...] * cot[p]).astype(BF16)
        gmix[p] = grad_mixed
        gact[...] = lax.dot_general(
            grad_mixed, w_out_ref[...], (((1,), (1,)), ((), ())), preferred_element_type=F32
        )

        @pl.loop(0, Wp // 16)
        def _(c):
            q = pl.ds(pl.multiple_of(c * 16, 16), 16)
            h = hid[q] + b_in_ref[...]
            h2 = h * h
            th = jnp.tanh(ROOT_TERM * (h + CUBIC * h2 * h))
            half = 0.5 * (1.0 + th)
            act[p, q] = (h * half).astype(BF16)
            slope = half + 0.5 * h * (1.0 - th * th) * ROOT_TERM * (1.0 + 3.0 * CUBIC * h2)
            grad_hidden = (gact[q] * slope).astype(BF16)
            gh[p, q] = grad_hidden
            wide = grad_hidden.astype(F32)
            bsum[...] += wide[0:8] + wide[8:16]

        mixed = jnp.dot(act[p], w_out_ref[...], preferred_element_type=F32) + b_out_ref[...]
        out_ref[p] = (xo[p].astype(F32) + ocean * ls_ref[...] * mixed).astype(BF16)[0:W]
        grad_normed = lax.dot_general(
            gh[p], w_in_ref[...], (((1,), (1,)), ((), ())), preferred_element_type=F32
        )
        unit = gf[p]
        scaled = grad_normed * gain_ref[...]
        grad_conv = rstd * (
            scaled
            - jnp.mean(scaled, axis=-1, keepdims=True)
            - unit * jnp.mean(scaled * unit, axis=-1, keepdims=True)
        )
        rounded = grad_conv.astype(BF16)
        gb[p] = rounded
        chan[0:1] += rowsum(rounded.astype(F32))
        chan[1:2] += rowsum(grad_normed * unit)
        chan[2:3] += rowsum(grad_normed)
        chan[3:4] += rowsum(gmix[p].astype(F32))
        chan[4:5] += rowsum(ocean * cot[p] * mixed)

    @pl.loop(1, H - 1)
    def _(p):
        pointwise(p)

    halo_start(*g_side, [1, 2], [1, 0])
    halo_arrive(*x_side, [2], [0])
    halo_spread(x_top, x_bot, xs, [2], [0])
    conv(xs, [0, H + 5], False, False)

    @pl.loop(0, 2)
    def _(k):
        pointwise(k * (H - 1))

    halo_start(*g_side, [0], [2])

    flat = H * Wp
    tiles = part.shape[0] * part.shape[1] * part.shape[2] * part.shape[3]
    T = part.shape[3]
    d_in = lax.dot_general(
        normed[...].reshape(flat, C),
        gh[...].reshape(flat, HID),
        (((0,), (0,)), ((), ())),
        preferred_element_type=F32,
    )
    per = C // 16
    for cb in range(HID // C):
        for rb in range(per):
            k = cb * per + rb
            part[k // (tiles // 2), k // (tiles // 4) % 2, k // T % m, k % T, 0:16] = d_in[
                rb * 16 : rb * 16 + 16, cb * C : cb * C + C
            ].astype(BF16)
    d_out = lax.dot_general(
        gmix[...].reshape(flat, C),
        act[...].reshape(flat, HID),
        (((0,), (0,)), ((), ())),
        preferred_element_type=F32,
    ).T
    for k in range(tiles):
        part[k // (tiles // 2), k // (tiles // 4) % 2, k // T % m, k % T, 16:32] = d_out[
            k * 16 : k * 16 + 16
        ].astype(BF16)

    step1 = remote(part.at[1 - d], r1, send_sem.at[0], recv_sem.at[0], core)
    step1.start()

    for j in range(7):

        def tap_terms(c, sums):
            q = pl.ds(c * 2, 2)
            cells16 = pl.ds(pl.multiple_of(c * 16, 16), 16)
            grads = [gb[p, cells16].astype(F32).reshape(2, 8, C) for p in range(H)]
            sums = list(sums)
            for r in range(H + 6):
                cells = xs[j, r, q]
                for p in range(H):
                    i = r - p
                    if 0 <= i < 7:
                        term = cells * grads[p]
                        sums[i] = sums[i] + (term[0] + term[1])
            return tuple(sums)

        sums = lax.fori_loop(0, B // 2, tap_terms, tuple(jnp.zeros((8, C), F32) for _ in range(7)))
        for i in range(7):
            k = i * 7 + j
            sm[k // 32, k % 32 : k % 32 + 1] = rowsum(sums[i])
    step1.wait()
    r1[...] = (part[d].astype(F32) + r1[...].astype(F32)).astype(BF16)
    step2 = remote(r1.at[1 - yy], r2, send_sem.at[1], recv_sem.at[1], beside)
    step2.start()

    hidden_sum = rowsum(bsum[...])
    for k in range(HID // C):
        sm[1, 17 + k : 18 + k] = hidden_sum[:, k * C : k * C + C]
    sm[1, 21:26] = chan[0:5]
    sm[1, 26:32] = jnp.zeros((6, C), F32)

    small1 = remote(sm.at[1 - d], s1, send_sem.at[4], recv_sem.at[4], core)
    small1.start()

    own_spread(gb, xs)
    conv(xs, own_rows, True, True)

    step2.wait()
    r2[...] = (r1[yy].astype(F32) + r2[...].astype(F32)).astype(BF16)
    step3 = [
        remote(r2.at[lax.rem(zz + k, m)], r3.at[k - 1], z_send.at[k - 1], z_recv.at[k - 1], zpeer[k])
        for k in range(1, m)
    ]
    for copy in step3:
        copy.start()
    small1.wait()
    s2[...] = sm[d] + s1[...]
    small2 = remote(s2, s3, send_sem.at[5], recv_sem.at[5], beside)
    small2.start()

    halo_arrive(*g_side, [1, 2], [1, 0])
    halo_spread(g_top, g_bot, xs, [1, 2], [1, 0])

    for copy in step3:
        copy.wait()
    total = r2[zz].astype(F32)
    for k in range(m - 1):
        total = total + r3[k].astype(F32)
    whole[d, yy, zz] = (total * scale).astype(BF16)
    mine = whole.at[d, yy, zz]
    step4 = [
        remote(mine, mine, z_send.at[m - 2 + k], z_recv.at[m - 2 + k], zpeer[k])
        for k in range(1, m)
    ]
    for copy in step4:
        copy.start()
    small2.wait()
    s5[zz] = s2[...] + s3[...]
    small3 = [
        remote(s5.at[zz], s5.at[zz], z_send.at[2 * m - 3 + k], z_recv.at[2 * m - 3 + k], zpeer[k])
        for k in range(1, m)
    ]
    for copy in small3:
        copy.start()

    conv(xs, [0, 1, H + 4, H + 5], True, False)
    halo_arrive(*g_side, [0], [2])
    halo_spread(g_top, g_bot, xs, [0], [2])
    conv(xs, [2, H + 3], True, False)
    halo_sent(*x_side)
    halo_sent(*g_side)

    for copy in step4:
        copy.wait()
    step5 = remote(
        whole.at[d, yy], whole.at[d, yy], send_sem.at[2], recv_sem.at[2], beside
    )
    step5.start()
    for copy in small3:
        copy.wait()
    small_total = s5[0]
    for k in range(1, m):
        small_total = small_total + s5[k]
    s6[d] = small_total * scale
    small4 = remote(s6.at[d], s6.at[d], send_sem.at[6], recv_sem.at[6], core)
    small4.start()
    for p in range(H):
        igrad_ref[p] = (cot[p] + acc[p].reshape(Wp, C)).astype(BF16)[0:W]
    step5.wait()
    step6 = remote(whole.at[d], whole.at[d], send_sem.at[3], recv_sem.at[3], core)
    step6.start()
    small4.wait()
    rows = s6[...].reshape(64, C)
    for i in range(7):
        kgrad_ref[i] = rows[i * 7 : i * 7 + 7]
    for k in range(HID // C):
        bgrad_ref[0:1, k * C : k * C + C] = rows[49 + k : 50 + k]
    chan_ref[...] = rows[49 + HID // C : 54 + HID // C]
    step6.wait()
    for cb in range(HID // C):
        for rb in range(per):
            k = cb * per + rb
            wi_ref[rb * 16 : rb * 16 + 16, cb * C : cb * C + C] = whole[
                k // (tiles // 2), k // (tiles // 4) % 2, k // T % m, k % T, 0:16
            ].astype(F32)
    for k in range(tiles):
        wo_ref[k * 16 : k * 16 + 16] = whole[
            k // (tiles // 2), k // (tiles // 4) % 2, k // T % m, k % T, 16:32
        ].astype(F32)


def per_device(
    n,
    draws,
    inputs,
    land_mask,
    kernel,
    conv_bias,
    norm_gain,
    norm_bias,
    w_in,
    b_in,
    w_out,
    b_out,
    layer_scale,
    cotangent,
):
    _, H, W, C = inputs.shape
    HID = w_in.shape[1]
    Wp = (W + 15) // 16 * 16
    B = Wp // 8
    m = n // 2
    T = HID // 16 // (2 * n)
    scale = float(1.0 / (draws * H * n * W) ** 0.5)
    ocean = jnp.broadcast_to(
        jnp.pad(land_mask, ((0, 0), (0, Wp - W))).astype(BF16)[:, :, None], (H, Wp, C)
    )
    taps = jnp.broadcast_to(kernel.reshape(49, 1, C), (49, 8, C))
    vm = pl.BlockSpec(memory_space=pltpu.VMEM)
    scratch = [
        ((H, Wp, C), BF16),
        ((3, Wp, C), BF16),
        ((3, Wp, C), BF16),
        ((H, Wp, C), F32),
        ((Wp + 16, C), F32),
        ((7, H + 6, B, 8, C), F32),
        ((H, B, 8, C), F32),
        ((Wp, HID), F32),
        ((Wp, HID), F32),
        ((H, Wp, HID), BF16),
        ((H, Wp, HID), BF16),
        ((H, Wp, C), BF16),
        ((H, Wp, C), BF16),
        ((H, Wp, C), BF16),
        ((3, Wp, C), BF16),
        ((3, Wp, C), BF16),
        ((H, Wp, C), F32),
        ((8, HID), F32),
        ((8, C), F32),
        ((2, 2, m, T, 32, C), BF16),
        ((2, m, T, 32, C), BF16),
        ((m, T, 32, C), BF16),
        ((m - 1, T, 32, C), BF16),
        ((2, 2, m, T, 32, C), BF16),
        ((2, 32, C), F32),
        ((32, C), F32),
        ((32, C), F32),
        ((32, C), F32),
        ((m, 32, C), F32),
        ((2, 32, C), F32),
    ]
    output, input_grad, w_in_grad, w_out_grad, kernel_grad, b_in_grad, channel = pl.pallas_call(
        functools.partial(block_kernel, n, scale),
        out_shape=(
            jax.ShapeDtypeStruct((H, W, C), BF16),
            jax.ShapeDtypeStruct((H, W, C), BF16),
            jax.ShapeDtypeStruct((C, HID), F32),
            jax.ShapeDtypeStruct((HID, C), F32),
            jax.ShapeDtypeStruct((7, 7, C), F32),
            jax.ShapeDtypeStruct((1, HID), F32),
            jax.ShapeDtypeStruct((5, C), F32),
        ),
        in_specs=[vm] * 12,
        out_specs=[vm] * 7,
        scratch_shapes=[pltpu.VMEM(shape, dtype) for shape, dtype in scratch]
        + [
            pltpu.SemaphoreType.DMA((12,)),
            pltpu.SemaphoreType.DMA((12,)),
            pltpu.SemaphoreType.DMA((7,)),
            pltpu.SemaphoreType.DMA((7,)),
            pltpu.SemaphoreType.DMA((3 * (m - 1),)),
            pltpu.SemaphoreType.DMA((3 * (m - 1),)),
        ],
        compiler_params=pltpu.CompilerParams(
            collective_id=0, has_side_effects=True, vmem_limit_bytes=60 * 1024 * 1024
        ),
    )(
        inputs[0],
        cotangent[0],
        ocean,
        taps,
        conv_bias[None],
        norm_gain[None],
        norm_bias[None],
        w_in,
        b_in[None],
        w_out,
        b_out[None],
        layer_scale[None],
    )
    return (
        output[None],
        input_grad[None],
        kernel_grad,
        w_in_grad,
        w_out_grad,
        b_in_grad[0],
        channel,
    )


def solution(mesh):
    field = P(("group", "draw"), "tile", None, None)
    placed = (field, P("tile", None)) + (P(),) * 9 + (field,)
    return jax.shard_map(
        functools.partial(per_device, mesh.shape["tile"], mesh.shape["draw"]),
        mesh=mesh,
        in_specs=placed,
        out_specs=(
            field,
            field,
            P("group", None, None),
            P("group", None),
            P("group", None),
            P("group"),
            P("group", None),
        ),
        check_vma=False,
    )
```
